32 devices in a mesh: node: 4 (over z), local: 8 (over y, x, core).
Axes of the slice: x: 2, y: 2, z: 4, core: 2. Of those that a mesh axis runs over, the one named last changes fastest.
Arguments:
- tokens: bfloat16 [32, 3584], P(('node', 'local')), may hold values from -6 to 6
- out_grad: bfloat16 [32, 3584], P(('node', 'local')), may hold values from -2 to 2
- gate_prob: bfloat16 [32, 8], P(('node', 'local')), may hold values from 0.099609375 to 1
- dest_node: int32 [32, 8], P(('node', 'local')), may hold values from 0 to 3, as said below
- w_gate: bfloat16 [32, 3584, 1024], P(('node', 'local')), may hold values from -0.09375 to 0.09375
- w_up: bfloat16 [32, 3584, 1024], P(('node', 'local')), may hold values from -0.09375 to 0.09375
- w_down: bfloat16 [32, 1024, 3584], P(('node', 'local')), may hold values from -0.1875 to 0.1875
Outputs:
- in_grad: bfloat16 [32, 3584], P(('node', 'local'))
- gate_grad: float32 [32, 8], P(('node', 'local'))
The draws below stay inside these ranges and needn't reach their ends.
Inputs may be any that keep to these rules, and one draw needn't show every extreme that they name: `dest_node`: columns 2 * g and 2 * g + 1 of a row are equal, so a token names at most half of 8 node groups, two experts in each. Among the 8 tokens of one node group, at most 4 name the same node group in one column; for each pair of columns one node group, the same for all source groups, is named by exactly 4 of them.
All inputs are finite; a program needn't handle non-finite values.
Results may differ from the reference program's by a relative error of at most 0.006.
Values may be sent and summed in bfloat16 or wider, within the bound.
A program may use at most 64 MiB of HBM per device.

```python
import math
import jax
import jax.numpy as jnp
from jax import lax

D = 3584
FF = 1024
EXP_NODE = 8
TOK_DEV = 1
SHARDS = 1
FF_DEV = 1024
CAP = 4
EXPERTS = 32
TOKENS = 32
N_NODE = 4
N_LOCAL = 8


def draw_dest_node(key, part):
    key = jax.random.fold_in(key, 7)
    members = N_LOCAL * TOK_DEV
    pairs = EXP_NODE // 2
    capacity = 2 * members // N_NODE
    key_busy, key_perm = jax.random.split(key)
    busy = jax.random.randint(key_busy, (1, pairs, 1), 0, N_NODE)
    perm_keys = jax.random.split(key_perm, N_NODE * pairs)
    ranks = jax.vmap(partial_permutation(members))(perm_keys).reshape(N_NODE, pairs, members)
    spill = jnp.maximum(ranks - capacity, 0) % max(N_NODE - 1, 1)
    others = (busy + 1 + spill) % N_NODE
    chosen = jnp.where(ranks < capacity, busy, others)
    chosen = jnp.repeat(chosen, 2, axis=1)
    return chosen.transpose(0, 2, 1).reshape(N_NODE * members, EXP_NODE).astype(jnp.int32)


def partial_permutation(members):

    def permute(single_key):
        return jax.random.permutation(single_key, members)
    return permute


def block_levels(stream_key, dims, cuts, least, high):
    factor_of = 1.0
    for axis_at, blocks in cuts:
        draws = jax.random.uniform(jax.random.fold_in(jax.random.fold_in(stream_key, 6), axis_at), (blocks,), jnp.float32, least / len(cuts), high / len(cuts))
        factor_of = factor_of * jnp.repeat(jnp.exp(draws), dims[axis_at] // blocks).reshape((-1,) + (1,) * (len(dims) - 1 - axis_at))
    return factor_of


def centred(rng, shape, width, bound, pieces=(), kind=jnp.bfloat16):
    drawn = jax.random.normal(rng, shape, jnp.float32) * width
    if len(pieces) > 0:
        drawn = block_levels(rng, shape, pieces, -0.22, 0.18) * drawn
    return jnp.clip(drawn, min=-bound, max=bound).astype(kind)


def setup_inputs(seed: int = 0) -> dict:
    arg_keys = jax.random.split(jax.random.key(seed), 8)
    tokens = centred(arg_keys[0], (TOKENS, D), 1.0, 6.0, ((0, 32),))
    out_grad = centred(arg_keys[1], (TOKENS, D), 0.3, 2.0, ((0, 32),))
    gate_prob = jnp.clip(jnp.exp(math.log(1.0) - 2.306499 * jax.random.uniform(arg_keys[2], (TOKENS, EXP_NODE), jnp.float32) ** block_levels(arg_keys[2], (TOKENS, EXP_NODE), ((0, 32),), -0.2, 0.2)), 0.099609375, 1.0).astype(jnp.bfloat16)
    dest_node = draw_dest_node(jax.random.fold_in(arg_keys[7], 71), 0)
    w_gate = centred(arg_keys[4], (EXPERTS * SHARDS, D, FF_DEV), D ** -0.5, 0.09375, ((0, 32),))
    w_up = centred(arg_keys[5], (EXPERTS * SHARDS, D, FF_DEV), D ** -0.5, 0.09375, ((0, 32),))
    w_down = centred(arg_keys[6], (EXPERTS * SHARDS, FF_DEV, D), FF ** -0.5, 0.1875, ((0, 32),))
    return dict(tokens=tokens, out_grad=out_grad, gate_prob=gate_prob, dest_node=dest_node, w_gate=w_gate, w_up=w_up, w_down=w_down)


def expert_terms(rows_x, rows_dy, rows_gate, weight_gate, weight_up, weight_down):
    contract = (((1,), (1,)), ((), ()))
    pre_gate = jnp.dot(rows_x, weight_gate, preferred_element_type=jnp.float32)
    pre_up = jnp.dot(rows_x, weight_up, preferred_element_type=jnp.float32)
    logistic = jax.nn.sigmoid(pre_gate)
    swished = pre_gate * logistic
    hidden = swished * pre_up
    back_hidden = lax.dot_general(rows_dy, weight_down, contract, preferred_element_type=jnp.float32)
    gate_terms = jnp.sum(hidden * back_hidden, axis=1)
    scaled = rows_gate[:, None] * back_hidden
    grad_gate = (scaled * pre_up * logistic * (1.0 + pre_gate * (1.0 - logistic))).astype(jnp.bfloat16)
    grad_up = (scaled * swished).astype(jnp.bfloat16)
    input_terms = lax.dot_general(grad_gate, weight_gate, contract, preferred_element_type=jnp.float32)
    input_terms = input_terms + lax.dot_general(grad_up, weight_up, contract, preferred_element_type=jnp.float32)
    return input_terms, gate_terms


def reference(tokens, out_grad, gate_prob, dest_node, w_gate, w_up, w_down):
    experts = N_NODE * EXP_NODE
    limit = N_NODE * CAP
    full_gate = w_gate.reshape(experts, SHARDS, D, FF_DEV).transpose(0, 2, 1, 3).reshape(experts, D, FF)
    full_up = w_up.reshape(experts, SHARDS, D, FF_DEV).transpose(0, 2, 1, 3).reshape(experts, D, FF)
    full_down = w_down.reshape(experts, FF, D)
    pad_x = jnp.concatenate([tokens, jnp.zeros((1, D), tokens.dtype)], 0)
    pad_dy = jnp.concatenate([out_grad, jnp.zeros((1, D), out_grad.dtype)], 0)
    pad_gate = jnp.concatenate([gate_prob.astype(jnp.float32), jnp.zeros((1, EXP_NODE), jnp.float32)], 0)

    def add_expert(expert, carry):
        acc_x, acc_gate = carry
        column = expert % EXP_NODE
        group_id = expert // EXP_NODE
        chosen = jnp.take(dest_node, column, axis=1) == group_id
        index = jnp.nonzero(chosen, size=limit, fill_value=TOKENS)[0].astype(jnp.int32)
        rows_gate = jnp.take(jnp.take(pad_gate, column, axis=1), index)
        input_terms, gate_terms = expert_terms(pad_x[index], pad_dy[index], rows_gate,
                                               full_gate[expert], full_up[expert], full_down[expert])
        acc_x = acc_x.at[index].add(input_terms)
        onehot = (jnp.arange(EXP_NODE) == column).astype(acc_gate.dtype)
        acc_gate = acc_gate.at[index].add(gate_terms[:, None] * onehot[None, :])
        return acc_x, acc_gate

    start = (jnp.zeros((TOKENS + 1, D), jnp.float32), jnp.zeros((TOKENS + 1, EXP_NODE), jnp.float32))
    acc_x, acc_gate = lax.fori_loop(0, experts, add_expert, start)
    return acc_x[:TOKENS].astype(jnp.bfloat16), acc_gate[:TOKENS]
```

```python
import functools

import jax
import jax.numpy as jnp
from jax import lax
from jax.experimental import pallas as pl
from jax.experimental.pallas import tpu as pltpu
from jax.sharding import PartitionSpec as P

MESH = pl.DeviceIdType.MESH
LANES = 128
TILE = 256
HALVES = 2


def expert_terms(rows_x, rows_dy, rows_gate, weight_gate, weight_up, weight_down):
    contract = (((1,), (1,)), ((), ()))
    pre_gate = jnp.dot(rows_x, weight_gate, preferred_element_type=jnp.float32)
    pre_up = jnp.dot(rows_x, weight_up, preferred_element_type=jnp.float32)
    logistic = jax.nn.sigmoid(pre_gate)
    swished = pre_gate * logistic
    hidden = swished * pre_up
    back_hidden = lax.dot_general(
        rows_dy, weight_down, contract, preferred_element_type=jnp.float32
    )
    gate_terms = jnp.sum(hidden * back_hidden, axis=1)
    scaled = rows_gate[:, None] * back_hidden
    grad_gate = (scaled * pre_up * logistic * (1.0 + pre_gate * (1.0 - logistic))).astype(
        jnp.bfloat16
    )
    grad_up = (scaled * swished).astype(jnp.bfloat16)
    input_terms = lax.dot_general(
        grad_gate, weight_gate, contract, preferred_element_type=jnp.float32
    )
    input_terms = input_terms + lax.dot_general(
        grad_up, weight_up, contract, preferred_element_type=jnp.float32
    )
    return (input_terms, gate_terms)


def routed(tokens, out_grad, gate_prob, dest_node, w_gate, w_up, w_down):
    node_count = lax.axis_size("node")
    local_count = lax.axis_size("local")
    local_id = lax.axis_index("local")
    width = tokens.shape[1]
    experts_here = gate_prob.shape[1]
    shards = local_count // experts_here
    column = local_id // shards
    pick_float = (jnp.arange(experts_here) == column).astype(jnp.float32)
    dest_half = dest_node.astype(jnp.bfloat16)
    home_x, home_dy, home_gate, home_dest = (
        lax.all_gather(tokens, "local", axis=0, tiled=True),
        lax.all_gather(out_grad, "local", axis=0, tiled=True),
        lax.all_gather(gate_prob, "local", axis=0, tiled=True),
        lax.all_gather(dest_half, "local", axis=0, tiled=True),
    )
    members = home_x.shape[0]
    capacity = 2 * members // node_count
    slots = node_count * capacity
    target = jnp.sum(home_dest.astype(jnp.float32) * pick_float[None, :], axis=1).astype(jnp.int32)
    onehot_dest = (target[:, None] == jnp.arange(node_count)[None, :]).astype(jnp.int32)
    before = jnp.cumsum(onehot_dest, axis=0) - onehot_dest
    position = target * capacity + jnp.sum(before * onehot_dest, axis=1)
    place_half = (jnp.arange(slots)[:, None] == position[None, :]).astype(jnp.bfloat16)
    send_x = jnp.dot(place_half, home_x, preferred_element_type=jnp.float32).astype(jnp.bfloat16)
    send_dy = jnp.dot(place_half, home_dy, preferred_element_type=jnp.float32).astype(jnp.bfloat16)
    send_gate = jnp.dot(place_half, home_gate, preferred_element_type=jnp.float32).astype(
        jnp.bfloat16
    )

    def over_node(rows):
        return lax.all_to_all(
            rows.reshape(node_count, -1, rows.shape[1]),
            "node",
            split_axis=0,
            concat_axis=0,
            tiled=True,
        ).reshape(rows.shape)

    part_x, part_dy, part_gate = over_node(send_x), over_node(send_dy), over_node(send_gate)
    rows_gate = jnp.sum(part_gate.astype(jnp.float32) * pick_float[None, :], axis=1)
    input_terms, gate_terms = expert_terms(
        part_x, part_dy, rows_gate, w_gate[0], w_up[0], w_down[0]
    )
    gate_cols = gate_terms[:, None] * pick_float[None, :]
    back_x, back_gate = over_node(input_terms), over_node(gate_cols)
    term_x = jnp.take(back_x, position, axis=0)
    term_gate = jnp.take(back_gate, position, axis=0)
    summed_x, summed_gate = (
        lax.psum_scatter(term_x, "local", scatter_dimension=0, tiled=True),
        lax.psum_scatter(term_gate, "local", scatter_dimension=0, tiled=True),
    )
    return (summed_x.astype(jnp.bfloat16), summed_gate)


def dot_nt(a, b):
    return lax.dot_general(a, b, (((1,), (1,)), ((), ())), preferred_element_type=jnp.float32)


def fused_kernel(
    nodes,
    locals_,
    tok_ref,
    dy_ref,
    prob_ref,
    dest_ref,
    wg_hbm,
    wu_hbm,
    wd_hbm,
    out_ref,
    gate_ref,
    wg,
    wu,
    wd,
    stage,
    gath,
    wide,
    x_rows,
    dy_rows,
    dg,
    du,
    terms,
    send1,
    recv1,
    part,
    recv2,
    w_sem,
    zs,
    zr,
    cs,
    cr,
    ks,
    kr,
    ls,
    lr,
    bs,
    br,
):
    f32, bf16 = jnp.float32, jnp.bfloat16
    node, me = lax.axis_index("node"), lax.axis_index("local")
    chips = locals_ // 2
    chip, core = me // 2, me % 2
    sibling = chip * 2 + (1 - core)
    width = tok_ref.shape[1]
    units = wg.shape[1]
    half = width // HALVES
    rows = half // LANES
    padded = send1.shape[2] // nodes
    count = nodes * locals_

    loads = [
        pltpu.make_async_copy(src.at[0], dst, w_sem.at[i])
        for i, (src, dst) in enumerate(((wg_hbm, wg), (wu_hbm, wu), (wd_hbm, wd)))
    ]
    barrier = pltpu.get_barrier_semaphore()
    for k in range(1, nodes):
        pl.semaphore_signal(
            barrier, inc=1, device_id=((node + k) % nodes, me), device_id_type=MESH
        )
    for k in range(1, locals_):
        pl.semaphore_signal(
            barrier, inc=1, device_id=(node, (me + k) % locals_), device_id_type=MESH
        )
    for load in loads:
        load.start()

    stage[...] = jnp.zeros_like(stage)
    for at, ref in enumerate((tok_ref, dy_ref)):
        for h in range(HALVES):
            base = (at * HALVES + h) * padded
            for c in range(rows):
                lane = h * half + c * LANES
                stage[base + c : base + c + 1, :] = ref[:, lane : lane + LANES].astype(f32)
    experts = prob_ref.shape[1]
    stage[rows : rows + 1, 0:experts] = prob_ref[...].astype(f32)
    stage[rows + 1 : rows + 2, 0:experts] = dest_ref[...].astype(f32)
    gath[me, node] = stage[...].astype(bf16)
    pl.semaphore_wait(barrier, nodes - 1 + locals_ - 1)

    sent = []

    def send(src, dst, s_sem, r_sem, to):
        copy = pltpu.make_async_remote_copy(
            src_ref=src,
            dst_ref=dst,
            send_sem=s_sem,
            recv_sem=r_sem,
            device_id=to,
            device_id_type=MESH,
        )
        copy.start()
        sent.append(copy)

    def await_recv(ref, s_sem, r_sem):
        pltpu.make_async_remote_copy(
            src_ref=ref,
            dst_ref=ref,
            send_sem=s_sem,
            recv_sem=r_sem,
            device_id=(node, sibling),
            device_id_type=MESH,
        ).wait_recv()

    def spread(n, k):
        block = gath.at[me, n]
        for j in range(1, chips):
            to = ((chip + j) % chips) * 2 + core
            send(block, block, cs.at[k, j], cr.at[chip, n], (node, to))
        send(block, block, ks.at[k, 0], kr.at[chip, n], (node, sibling))

    own = gath.at[me, node]
    for k in range(1, nodes):
        send(own, own, zs.at[k], zr.at[node], ((node + k) % nodes, me))
    spread(node, 0)
    for k in range(1, nodes):
        n = (node + nodes - k) % nodes
        await_recv(gath.at[me, n], zs.at[0], zr.at[n])
        spread(n, k)
    for k in range(nodes):
        n = (node + nodes - k) % nodes
        for j in range(1, chips):
            other = (chip + chips - j) % chips
            block = gath.at[other * 2 + core, n]
            await_recv(block, cs.at[0, 0], cr.at[other, n])
            send(block, block, ks.at[k, j], kr.at[other, n], (node, sibling))
    for k in range(nodes):
        n = (node + nodes - k) % nodes
        for j in range(chips):
            other = (chip + chips - j) % chips
            await_recv(gath.at[other * 2 + 1 - core, n], ks.at[0, 0], kr.at[other, n])

    depth = 2 * HALVES * padded
    for l in range(locals_):
        for n in range(nodes):
            at = (l * nodes + n) * depth
            wide[at : at + depth, :] = gath[l, n].astype(f32)
    for at, ref in enumerate((x_rows, dy_rows)):
        for h in range(HALVES):
            for c in range(rows):
                lane = h * half + c * LANES
                first = (at * HALVES + h) * padded + c
                ref[:, lane : lane + LANES] = wide[pl.ds(first, count, stride=depth), :].astype(
                    bf16
                )
    lane_id = lax.broadcasted_iota(jnp.int32, (count, LANES), 1)
    mine = lane_id == me
    probs = wide[pl.ds(rows, count, stride=depth), :]
    dests = wide[pl.ds(rows + 1, count, stride=depth), :]
    prob = jnp.sum(jnp.where(mine, probs, 0.0), axis=1, keepdims=True)
    dest = jnp.sum(jnp.where(mine, dests, 0.0), axis=1, keepdims=True)
    here = dest == node.astype(f32)
    prob = jnp.where(here, prob, 0.0)

    for load in loads:
        load.wait()

    def hidden_tile(i, gate_sum):
        at = pl.ds(pl.multiple_of(i * TILE, TILE), TILE)
        pre_gate = jnp.dot(x_rows[...], wg[:, at], preferred_element_type=f32)
        pre_up = jnp.dot(x_rows[...], wu[:, at], preferred_element_type=f32)
        back = dot_nt(dy_rows[...], wd[at, :])
        logistic = jax.nn.sigmoid(pre_gate)
        swished = pre_gate * logistic
        gate_sum = gate_sum + jnp.sum(swished * pre_up * back, axis=1, keepdims=True)
        scaled = prob * back
        dg[:, at] = (scaled * pre_up * logistic * (1.0 + pre_gate * (1.0 - logistic))).astype(bf16)
        du[:, at] = (scaled * swished).astype(bf16)
        return gate_sum

    gate_sum = lax.fori_loop(0, units // TILE, hidden_tile, jnp.zeros((count, 1), f32))
    gate_row = jnp.where(mine & here, gate_sum, 0.0)
    gate_high = gate_row.astype(bf16).astype(f32)

    for h in range(HALVES):
        for extra in range(rows, padded):
            value = jnp.zeros((count, LANES), f32)
            if h == 0 and extra == rows:
                value = gate_high
            if h == 0 and extra == rows + 1:
                value = gate_row - gate_high
            terms[pl.ds(extra, count, stride=padded), :] = value

        def input_tile(i, _):
            at = pl.ds(pl.multiple_of(h * half + i * TILE, TILE), TILE)
            block = dot_nt(dg[...], wg[at, :]) + dot_nt(du[...], wu[at, :])
            for c in range(TILE // LANES):
                terms[pl.ds(i * (TILE // LANES) + c, count, stride=padded), :] = block[
                    :, c * LANES : (c + 1) * LANES
                ]
            return 0

        lax.fori_loop(0, half // TILE, input_tile, 0)
        for l in range(locals_):
            at = l * nodes * padded
            send1[h, l] = terms[at : at + nodes * padded, :].astype(bf16)
        for k in range(1, locals_):
            to = (me + k) % locals_
            send(send1.at[h, to], recv1.at[h, me], ls.at[h, k], lr.at[h, me], (node, to))

    for h in range(HALVES):
        total = send1[h, me].astype(f32)
        for k in range(1, locals_):
            source = (me + locals_ - k) % locals_
            await_recv(recv1.at[h, source], ls.at[h, 0], lr.at[h, source])
            total = total + recv1[h, source].astype(f32)
        for n in range(nodes):
            part[h, n] = total[n * padded : (n + 1) * padded]
        for k in range(1, nodes):
            to = (node + k) % nodes
            send(part.at[h, to], recv2.at[h, node], bs.at[h, k], br.at[h, node], (to, me))
    for h in range(HALVES):
        total = part[h, node]
        for k in range(1, nodes):
            source = (node + nodes - k) % nodes
            await_recv(recv2.at[h, source], bs.at[h, 0], br.at[h, source])
            total = total + recv2[h, source]
        for c in range(rows):
            lane = h * half + c * LANES
            out_ref[:, lane : lane + LANES] = total[c : c + 1].astype(bf16)
        if h == 0:
            gate_ref[...] = (total[rows : rows + 1] + total[rows + 1 : rows + 2])[:, 0:experts]
    for copy in sent:
        copy.wait_send()


def fused(nodes, locals_, tokens, out_grad, gate_prob, dest_node, w_gate, w_up, w_down):
    f32, bf16 = jnp.float32, jnp.bfloat16
    width, units = w_gate.shape[1:]
    count = nodes * locals_
    chips = locals_ // 2
    padded = padded_rows(width)
    depth = 2 * HALVES * padded
    vmem = pl.BlockSpec(memory_space=pltpu.VMEM)
    hbm = pl.BlockSpec(memory_space=pl.ANY)
    dma = pltpu.SemaphoreType.DMA
    return pl.pallas_call(
        functools.partial(fused_kernel, nodes, locals_),
        out_shape=(
            jax.ShapeDtypeStruct((1, width), bf16),
            jax.ShapeDtypeStruct(gate_prob.shape, f32),
        ),
        in_specs=[vmem] * 4 + [hbm] * 3,
        out_specs=(vmem, vmem),
        scratch_shapes=[
            pltpu.VMEM((width, units), bf16),
            pltpu.VMEM((width, units), bf16),
            pltpu.VMEM((units, width), bf16),
            pltpu.VMEM((depth, LANES), f32),
            pltpu.VMEM((locals_, nodes, depth, LANES), bf16),
            pltpu.VMEM((count * depth, LANES), f32),
            pltpu.VMEM((count, width), bf16),
            pltpu.VMEM((count, width), bf16),
            pltpu.VMEM((count, units), bf16),
            pltpu.VMEM((count, units), bf16),
            pltpu.VMEM((count * padded, LANES), f32),
            pltpu.VMEM((HALVES, locals_, nodes * padded, LANES), bf16),
            pltpu.VMEM((HALVES, locals_, nodes * padded, LANES), bf16),
            pltpu.VMEM((HALVES, nodes, padded, LANES), f32),
            pltpu.VMEM((HALVES, nodes, padded, LANES), f32),
            dma((3,)),
            dma((nodes,)),
            dma((nodes,)),
            dma((nodes, chips)),
            dma((chips, nodes)),
            dma((nodes, chips)),
            dma((chips, nodes)),
            dma((HALVES, locals_)),
            dma((HALVES, locals_)),
            dma((HALVES, nodes)),
            dma((HALVES, nodes)),
        ],
        compiler_params=pltpu.CompilerParams(
            collective_id=0, has_side_effects=True, vmem_limit_bytes=56 << 20
        ),
        cost_estimate=pl.CostEstimate(
            flops=10 * count * width * units,
            bytes_accessed=6 * width * units,
            transcendentals=count * units,
        ),
    )(tokens, out_grad, gate_prob, dest_node, w_gate, w_up, w_down)


def padded_rows(width):
    return -(-(width // HALVES // LANES + 2) // 16) * 16


def on_device(nodes, locals_, tokens, out_grad, gate_prob, dest_node, w_gate, w_up, w_down):
    width, units = w_gate.shape[1:]
    weights = 6 * width * units
    rows = nodes * locals_ * 2 * HALVES * padded_rows(width) * LANES * 10
    small = (
        tokens.shape[0] == 1
        and gate_prob.shape[1] == locals_
        and locals_ % 2 == 0
        and width % (HALVES * TILE) == 0
        and units % TILE == 0
        and weights + rows < 40 << 20
    )
    plan = functools.partial(fused, nodes, locals_) if small else routed
    return plan(tokens, out_grad, gate_prob, dest_node, w_gate, w_up, w_down)


def solution(mesh):
    split = ("node", "local")
    return jax.shard_map(
        functools.partial(on_device, mesh.shape["node"], mesh.shape["local"]),
        mesh=mesh,
        in_specs=(P(split, None),) * 4 + (P(split, None, None),) * 3,
        out_specs=(P(split, None), P(split, None)),
        check_vma=False,
    )
```

```python
import functools

import jax
import jax.numpy as jnp
from jax import lax
from jax.experimental import pallas as pl
from jax.experimental.pallas import tpu as pltpu
from jax.sharding import PartitionSpec as P

MESH = pl.DeviceIdType.MESH
LANES = 128
TILE = 256
HALVES = 2


def expert_terms(rows_x, rows_dy, rows_gate, weight_gate, weight_up, weight_down):
    contract = (((1,), (1,)), ((), ()))
    pre_gate = jnp.dot(rows_x, weight_gate, preferred_element_type=jnp.float32)
    pre_up = jnp.dot(rows_x, weight_up, preferred_element_type=jnp.float32)
    logistic = jax.nn.sigmoid(pre_gate)
    swished = pre_gate * logistic
    hidden = swished * pre_up
    back_hidden = lax.dot_general(
        rows_dy, weight_down, contract, preferred_element_type=jnp.float32
    )
    gate_terms = jnp.sum(hidden * back_hidden, axis=1)
    scaled = rows_gate[:, None] * back_hidden
    grad_gate = (scaled * pre_up * logistic * (1.0 + pre_gate * (1.0 - logistic))).astype(
        jnp.bfloat16
    )
    grad_up = (scaled * swished).astype(jnp.bfloat16)
    input_terms = lax.dot_general(
        grad_gate, weight_gate, contract, preferred_element_type=jnp.float32
    )
    input_terms = input_terms + lax.dot_general(
        grad_up, weight_up, contract, preferred_element_type=jnp.float32
    )
    return (input_terms, gate_terms)


def routed(tokens, out_grad, gate_prob, dest_node, w_gate, w_up, w_down):
    node_count = lax.axis_size("node")
    local_count = lax.axis_size("local")
    local_id = lax.axis_index("local")
    width = tokens.shape[1]
    experts_here = gate_prob.shape[1]
    shards = local_count // experts_here
    column = local_id // shards
    pick_float = (jnp.arange(experts_here) == column).astype(jnp.float32)
    dest_half = dest_node.astype(jnp.bfloat16)
    home_x, home_dy, home_gate, home_dest = (
        lax.all_gather(tokens, "local", axis=0, tiled=True),
        lax.all_gather(out_grad, "local", axis=0, tiled=True),
        lax.all_gather(gate_prob, "local", axis=0, tiled=True),
        lax.all_gather(dest_half, "local", axis=0, tiled=True),
    )
    members = home_x.shape[0]
    capacity = 2 * members // node_count
    slots = node_count * capacity
    target = jnp.sum(home_dest.astype(jnp.float32) * pick_float[None, :], axis=1).astype(jnp.int32)
    onehot_dest = (target[:, None] == jnp.arange(node_count)[None, :]).astype(jnp.int32)
    before = jnp.cumsum(onehot_dest, axis=0) - onehot_dest
    position = target * capacity + jnp.sum(before * onehot_dest, axis=1)
    place_half = (jnp.arange(slots)[:, None] == position[None, :]).astype(jnp.bfloat16)
    send_x = jnp.dot(place_half, home_x, preferred_element_type=jnp.float32).astype(jnp.bfloat16)
    send_dy = jnp.dot(place_half, home_dy, preferred_element_type=jnp.float32).astype(jnp.bfloat16)
    send_gate = jnp.dot(place_half, home_gate, preferred_element_type=jnp.float32).astype(
        jnp.bfloat16
    )

    def over_node(rows):
        return lax.all_to_all(
            rows.reshape(node_count, -1, rows.shape[1]),
            "node",
            split_axis=0,
            concat_axis=0,
            tiled=True,
        ).reshape(rows.shape)

    part_x, part_dy, part_gate = over_node(send_x), over_node(send_dy), over_node(send_gate)
    rows_gate = jnp.sum(part_gate.astype(jnp.float32) * pick_float[None, :], axis=1)
    input_terms, gate_terms = expert_terms(
        part_x, part_dy, rows_gate, w_gate[0], w_up[0], w_down[0]
    )
    gate_cols = gate_terms[:, None] * pick_float[None, :]
    back_x, back_gate = over_node(input_terms), over_node(gate_cols)
    term_x = jnp.take(back_x, position, axis=0)
    term_gate = jnp.take(back_gate, position, axis=0)
    summed_x, summed_gate = (
        lax.psum_scatter(term_x, "local", scatter_dimension=0, tiled=True),
        lax.psum_scatter(term_gate, "local", scatter_dimension=0, tiled=True),
    )
    return (summed_x.astype(jnp.bfloat16), summed_gate)


def dot_nt(a, b):
    return lax.dot_general(a, b, (((1,), (1,)), ((), ())), preferred_element_type=jnp.float32)


def fused_kernel(
    nodes,
    locals_,
    tok_ref,
    dy_ref,
    prob_ref,
    dest_ref,
    wg_hbm,
    wu_hbm,
    wd_hbm,
    out_ref,
    gate_ref,
    wg,
    wu,
    wd,
    stage,
    gath_x,
    gath_dy,
    wide,
    rows_ref,
    pre_g,
    pre_u,
    dg,
    du,
    terms,
    send1,
    recv1,
    part,
    recv2,
    w_sem,
    zs,
    zr,
    cs,
    cr,
    ks,
    kr,
    ds,
    dr,
    ls,
    lr,
    bs,
    br,
):
    f32, bf16 = jnp.float32, jnp.bfloat16
    node, me = lax.axis_index("node"), lax.axis_index("local")
    chips = locals_ // 2
    chip, core = me // 2, me % 2
    width = tok_ref.shape[1]
    units = wg.shape[1]
    half = width // HALVES
    rows = half // LANES
    padded = send1.shape[3] // nodes
    count = nodes * locals_
    depth = HALVES * padded
    peers = [(j, side) for j in range(chips) for side in range(2) if (j, side) != (0, 0)]

    def ahead(j, side):
        return (node, ((chip + j) % chips) * 2 + (core if side == 0 else 1 - core))

    def back(j, side):
        return (node, ((chip + chips - j) % chips) * 2 + (core if side == 0 else 1 - core))

    loads = [
        pltpu.make_async_copy(src.at[0], dst, w_sem.at[i])
        for i, (src, dst) in enumerate(((wg_hbm, wg), (wu_hbm, wu), (wd_hbm, wd)))
    ]
    barrier = pltpu.get_barrier_semaphore()
    for k in range(1, nodes):
        pl.semaphore_signal(
            barrier, inc=1, device_id=((node + k) % nodes, me), device_id_type=MESH
        )
    for j, side in peers:
        pl.semaphore_signal(barrier, inc=1, device_id=ahead(j, side), device_id_type=MESH)
    for load in loads:
        load.start()

    experts = prob_ref.shape[1]
    for ref, gath in ((tok_ref, gath_x), (dy_ref, gath_dy)):
        stage[...] = jnp.zeros_like(stage)
        for h in range(HALVES):
            for c in range(rows):
                lane, at = h * half + c * LANES, h * padded + c
                stage[at : at + 1, :] = ref[:, lane : lane + LANES].astype(f32)
        if ref is tok_ref:
            stage[rows : rows + 1, 0:experts] = prob_ref[...].astype(f32)
            stage[rows + 1 : rows + 2, 0:experts] = dest_ref[...].astype(f32)
        gath[0, 0, 0] = stage[...].astype(bf16)
    pl.semaphore_wait(barrier, nodes - 1 + len(peers))

    sent = []

    def remote(src, dst, s_sem, r_sem, to):
        return pltpu.make_async_remote_copy(
            src_ref=src,
            dst_ref=dst,
            send_sem=s_sem,
            recv_sem=r_sem,
            device_id=to,
            device_id_type=MESH,
        )

    def send(src, dst, s_sem, r_sem, to):
        copy = remote(src, dst, s_sem, r_sem, to)
        copy.start()
        sent.append(copy)

    def await_recv(ref, s_sem, r_sem):
        remote(ref, ref, s_sem, r_sem, ahead(0, 1)).wait_recv()

    def across(k):
        for j in range(1, chips):
            send(gath_x.at[0, 0, k], gath_x.at[j, 0, k], cs.at[j, k], cr.at[j, k], ahead(j, 0))

    def sideways(j):
        send(gath_x.at[j, 0], gath_x.at[j, 1], ks.at[j], kr.at[j], ahead(0, 1))

    for at, gath in enumerate((gath_x, gath_dy)):
        for k in range(1, nodes):
            to = ((node + k) % nodes, me)
            send(gath.at[0, 0, 0], gath.at[0, 0, k], zs.at[at, k], zr.at[at, k], to)
        if at == 0:
            across(0)
    for k in range(1, nodes):
        await_recv(gath_x.at[0, 0, k], zs.at[0, 0], zr.at[0, k])
        across(k)
    sideways(0)
    for k in range(1, nodes):
        await_recv(gath_dy.at[0, 0, k], zs.at[0, 0], zr.at[1, k])
    for j, side in peers:
        send(
            gath_dy.at[0, 0],
            gath_dy.at[j, side],
            ds.at[j, side],
            dr.at[j, side],
            ahead(j, side),
        )
    for j in range(1, chips):
        for k in range(nodes):
            await_recv(gath_x.at[j, 0, k], cs.at[0, 0], cr.at[j, k])
        sideways(j)
    for j in range(chips):
        await_recv(gath_x.at[j, 1], ks.at[0], kr.at[j])

    def to_rows(gath):
        def widen(l, _):
            block = gath[l // 2, l % 2].astype(f32).reshape(nodes * depth, LANES)
            at = pl.multiple_of(l * (nodes * depth), nodes * depth)
            wide[pl.ds(at, nodes * depth), :] = block
            return 0

        lax.fori_loop(0, locals_, widen, 0)
        for h in range(HALVES):
            for c in range(rows):
                lane, first = h * half + c * LANES, h * padded + c
                rows_ref[:, lane : lane + LANES] = wide[
                    pl.ds(first, count, stride=depth), :
                ].astype(bf16)

    to_rows(gath_x)
    lane_id = lax.broadcasted_iota(jnp.int32, (count, LANES), 1)
    mine = lane_id == me
    probs = wide[pl.ds(rows, count, stride=depth), :]
    dests = wide[pl.ds(rows + 1, count, stride=depth), :]
    prob = jnp.sum(jnp.where(mine, probs, 0.0), axis=1, keepdims=True)
    dest = jnp.sum(jnp.where(mine, dests, 0.0), axis=1, keepdims=True)
    here = dest == node.astype(f32)
    prob = jnp.where(here, prob, 0.0)

    loads[0].wait()
    loads[1].wait()

    def forward_tile(i, _):
        at = pl.ds(pl.multiple_of(i * TILE, TILE), TILE)
        pre_g[:, at] = jnp.dot(rows_ref[...], wg[:, at], preferred_element_type=f32)
        pre_u[:, at] = jnp.dot(rows_ref[...], wu[:, at], preferred_element_type=f32)
        return 0

    lax.fori_loop(0, units // TILE, forward_tile, 0)

    for j, side in peers:
        await_recv(gath_dy.at[j, side], ds.at[0, 0], dr.at[j, side])
    to_rows(gath_dy)
    loads[2].wait()

    def hidden_tile(i, gate_sum):
        at = pl.ds(pl.multiple_of(i * TILE, TILE), TILE)
        pre_gate, pre_up = pre_g[:, at], pre_u[:, at]
        back_hidden = dot_nt(rows_ref[...], wd[at, :])
        logistic = jax.nn.sigmoid(pre_gate)
        swished = pre_gate * logistic
        gate_sum = gate_sum + jnp.sum(swished * pre_up * back_hidden, axis=1, keepdims=True)
        scaled = prob * back_hidden
        dg[:, at] = (scaled * pre_up * logistic * (1.0 + pre_gate * (1.0 - logistic))).astype(bf16)
        du[:, at] = (scaled * swished).astype(bf16)
        return gate_sum

    gate_sum = lax.fori_loop(0, units // TILE, hidden_tile, jnp.zeros((count, 1), f32))
    gate_row = jnp.where(mine & here, gate_sum, 0.0)
    gate_high = gate_row.astype(bf16).astype(f32)

    for h in range(HALVES):
        for extra in range(rows, padded):
            value = jnp.zeros((count, LANES), f32)
            if h == 0 and extra == rows:
                value = gate_high
            if h == 0 and extra == rows + 1:
                value = gate_row - gate_high
            terms[pl.ds(extra, count, stride=padded), :] = value

        def input_tile(i, _):
            at = pl.ds(pl.multiple_of(h * half + i * TILE, TILE), TILE)
            block = dot_nt(dg[...], wg[at, :]) + dot_nt(du[...], wu[at, :])
            for c in range(TILE // LANES):
                terms[pl.ds(i * (TILE // LANES) + c, count, stride=padded), :] = block[
                    :, c * LANES : (c + 1) * LANES
                ]
            return 0

        lax.fori_loop(0, half // TILE, input_tile, 0)
        for j in range(chips):
            for side in range(2):
                at = (j * 2 + side) * nodes * padded
                send1[h, j, side] = terms[at : at + nodes * padded, :].astype(bf16)
                if (j, side) != (0, 0):
                    send(
                        send1.at[h, j, side],
                        recv1.at[h, j, side],
                        ls.at[h, j, side],
                        lr.at[h, j, side],
                        back(j, side),
                    )

    for h in range(HALVES):
        total = send1[h, 0, 0].astype(f32)
        for j, side in peers:
            await_recv(recv1.at[h, j, side], ls.at[h, 0, 0], lr.at[h, j, side])
            total = total + recv1[h, j, side].astype(f32)
        for k in range(nodes):
            part[h, k] = total[k * padded : (k + 1) * padded]
        for k in range(1, nodes):
            to = ((node + nodes - k) % nodes, me)
            send(part.at[h, k], recv2.at[h, k], bs.at[h, k], br.at[h, k], to)
    for h in range(HALVES):
        total = part[h, 0]
        for k in range(1, nodes):
            await_recv(recv2.at[h, k], bs.at[h, 0], br.at[h, k])
            total = total + recv2[h, k]
        for c in range(rows):
            lane = h * half + c * LANES
            out_ref[:, lane : lane + LANES] = total[c : c + 1].astype(bf16)
        if h == 0:
            gate_ref[...] = (total[rows : rows + 1] + total[rows + 1 : rows + 2])[:, 0:experts]
    for copy in sent:
        copy.wait_send()


def fused(nodes, locals_, tokens, out_grad, gate_prob, dest_node, w_gate, w_up, w_down):
    f32, bf16 = jnp.float32, jnp.bfloat16
    width, units = w_gate.shape[1:]
    count = nodes * locals_
    chips = locals_ // 2
    padded = padded_rows(width)
    depth = HALVES * padded
    vmem = pl.BlockSpec(memory_space=pltpu.VMEM)
    hbm = pl.BlockSpec(memory_space=pl.ANY)
    dma = pltpu.SemaphoreType.DMA
    return pl.pallas_call(
        functools.partial(fused_kernel, nodes, locals_),
        out_shape=(
            jax.ShapeDtypeStruct((1, width), bf16),
            jax.ShapeDtypeStruct(gate_prob.shape, f32),
        ),
        in_specs=[vmem] * 4 + [hbm] * 3,
        out_specs=(vmem, vmem),
        scratch_shapes=[
            pltpu.VMEM((width, units), bf16),
            pltpu.VMEM((width, units), bf16),
            pltpu.VMEM((units, width), bf16),
            pltpu.VMEM((depth, LANES), f32),
            pltpu.VMEM((chips, 2, nodes, depth, LANES), bf16),
            pltpu.VMEM((chips, 2, nodes, depth, LANES), bf16),
            pltpu.VMEM((count * depth, LANES), f32),
            pltpu.VMEM((count, width), bf16),
            pltpu.VMEM((count, units), f32),
            pltpu.VMEM((count, units), f32),
            pltpu.VMEM((count, units), bf16),
            pltpu.VMEM((count, units), bf16),
            pltpu.VMEM((count * padded, LANES), f32),
            pltpu.VMEM((HALVES, chips, 2, nodes * padded, LANES), bf16),
            pltpu.VMEM((HALVES, chips, 2, nodes * padded, LANES), bf16),
            pltpu.VMEM((HALVES, nodes, padded, LANES), f32),
            pltpu.VMEM((HALVES, nodes, padded, LANES), f32),
            dma((3,)),
            dma((2, nodes)),
            dma((2, nodes)),
            dma((chips, nodes)),
            dma((chips, nodes)),
            dma((chips,)),
            dma((chips,)),
            dma((chips, 2)),
            dma((chips, 2)),
            dma((HALVES, chips, 2)),
            dma((HALVES, chips, 2)),
            dma((HALVES, nodes)),
            dma((HALVES, nodes)),
        ],
        compiler_params=pltpu.CompilerParams(
            collective_id=0, has_side_effects=True, vmem_limit_bytes=56 << 20
        ),
        cost_estimate=pl.CostEstimate(
            flops=10 * count * width * units,
            bytes_accessed=6 * width * units,
            transcendentals=count * units,
        ),
    )(tokens, out_grad, gate_prob, dest_node, w_gate, w_up, w_down)


def padded_rows(width):
    return -(-(width // HALVES // LANES + 2) // 16) * 16


def on_device(nodes, locals_, tokens, out_grad, gate_prob, dest_node, w_gate, w_up, w_down):
    width, units = w_gate.shape[1:]
    weights = 6 * width * units
    rows = nodes * locals_ * 2 * HALVES * padded_rows(width) * LANES * 10
    small = (
        tokens.shape[0] == 1
        and gate_prob.shape[1] == locals_
        and locals_ % 2 == 0
        and width % (HALVES * TILE) == 0
        and units % TILE == 0
        and weights + rows < 40 << 20
    )
    plan = functools.partial(fused, nodes, locals_) if small else routed
    return plan(tokens, out_grad, gate_prob, dest_node, w_gate, w_up, w_down)


def solution(mesh):
    split = ("node", "local")
    return jax.shard_map(
        functools.partial(on_device, mesh.shape["node"], mesh.shape["local"]),
        mesh=mesh,
        in_specs=(P(split, None),) * 4 + (P(split, None, None),) * 3,
        out_specs=(P(split, None), P(split, None)),
        check_vma=False,
    )
```

```python
import functools

import jax
import jax.numpy as jnp
from jax import lax
from jax.experimental import pallas as pl
from jax.experimental.pallas import tpu as pltpu
from jax.sharding import PartitionSpec as P

MESH = pl.DeviceIdType.MESH
LANES = 128
TILE = 256
HALVES = 2
PIECES = 2


def expert_terms(rows_x, rows_dy, rows_gate, weight_gate, weight_up, weight_down):
    contract = (((1,), (1,)), ((), ()))
    pre_gate = jnp.dot(rows_x, weight_gate, preferred_element_type=jnp.float32)
    pre_up = jnp.dot(rows_x, weight_up, preferred_element_type=jnp.float32)
    logistic = jax.nn.sigmoid(pre_gate)
    swished = pre_gate * logistic
    hidden = swished * pre_up
    back_hidden = lax.dot_general(
        rows_dy, weight_down, contract, preferred_element_type=jnp.float32
    )
    gate_terms = jnp.sum(hidden * back_hidden, axis=1)
    scaled = rows_gate[:, None] * back_hidden
    grad_gate = (scaled * pre_up * logistic * (1.0 + pre_gate * (1.0 - logistic))).astype(
        jnp.bfloat16
    )
    grad_up = (scaled * swished).astype(jnp.bfloat16)
    input_terms = lax.dot_general(
        grad_gate, weight_gate, contract, preferred_element_type=jnp.float32
    )
    input_terms = input_terms + lax.dot_general(
        grad_up, weight_up, contract, preferred_element_type=jnp.float32
    )
    return (input_terms, gate_terms)


def routed(tokens, out_grad, gate_prob, dest_node, w_gate, w_up, w_down):
    node_count = lax.axis_size("node")
    local_count = lax.axis_size("local")
    local_id = lax.axis_index("local")
    width = tokens.shape[1]
    experts_here = gate_prob.shape[1]
    shards = local_count // experts_here
    column = local_id // shards
    pick_float = (jnp.arange(experts_here) == column).astype(jnp.float32)
    dest_half = dest_node.astype(jnp.bfloat16)
    home_x, home_dy, home_gate, home_dest = (
        lax.all_gather(tokens, "local", axis=0, tiled=True),
        lax.all_gather(out_grad, "local", axis=0, tiled=True),
        lax.all_gather(gate_prob, "local", axis=0, tiled=True),
        lax.all_gather(dest_half, "local", axis=0, tiled=True),
    )
    members = home_x.shape[0]
    capacity = 2 * members // node_count
    slots = node_count * capacity
    target = jnp.sum(home_dest.astype(jnp.float32) * pick_float[None, :], axis=1).astype(jnp.int32)
    onehot_dest = (target[:, None] == jnp.arange(node_count)[None, :]).astype(jnp.int32)
    before = jnp.cumsum(onehot_dest, axis=0) - onehot_dest
    position = target * capacity + jnp.sum(before * onehot_dest, axis=1)
    place_half = (jnp.arange(slots)[:, None] == position[None, :]).astype(jnp.bfloat16)
    send_x = jnp.dot(place_half, home_x, preferred_element_type=jnp.float32).astype(jnp.bfloat16)
    send_dy = jnp.dot(place_half, home_dy, preferred_element_type=jnp.float32).astype(jnp.bfloat16)
    send_gate = jnp.dot(place_half, home_gate, preferred_element_type=jnp.float32).astype(
        jnp.bfloat16
    )

    def over_node(rows):
        return lax.all_to_all(
            rows.reshape(node_count, -1, rows.shape[1]),
            "node",
            split_axis=0,
            concat_axis=0,
            tiled=True,
        ).reshape(rows.shape)

    part_x, part_dy, part_gate = over_node(send_x), over_node(send_dy), over_node(send_gate)
    rows_gate = jnp.sum(part_gate.astype(jnp.float32) * pick_float[None, :], axis=1)
    input_terms, gate_terms = expert_terms(
        part_x, part_dy, rows_gate, w_gate[0], w_up[0], w_down[0]
    )
    gate_cols = gate_terms[:, None] * pick_float[None, :]
    back_x, back_gate = over_node(input_terms), over_node(gate_cols)
    term_x = jnp.take(back_x, position, axis=0)
    term_gate = jnp.take(back_gate, position, axis=0)
    summed_x, summed_gate = (
        lax.psum_scatter(term_x, "local", scatter_dimension=0, tiled=True),
        lax.psum_scatter(term_gate, "local", scatter_dimension=0, tiled=True),
    )
    return (summed_x.astype(jnp.bfloat16), summed_gate)


def dot_nt(a, b):
    return lax.dot_general(a, b, (((1,), (1,)), ((), ())), preferred_element_type=jnp.float32)


def fused_kernel(
    nodes,
    locals_,
    tok_ref,
    dy_ref,
    prob_ref,
    dest_ref,
    wg_hbm,
    wu_hbm,
    wd_hbm,
    out_ref,
    wg,
    wu,
    wd,
    stage,
    gath_x,
    gath_dy,
    wide,
    rows_ref,
    pre_g,
    pre_u,
    dg,
    du,
    terms,
    send1,
    recv1,
    part,
    recv2,
    w_sem,
    zs,
    zr,
    cs,
    cr,
    ks,
    kr,
    ds,
    dr,
    ls,
    lr,
    bs,
    br,
):
    f32, bf16 = jnp.float32, jnp.bfloat16
    node, me = lax.axis_index("node"), lax.axis_index("local")
    chips = locals_ // 2
    chip, core = me // 2, me % 2
    width = tok_ref.shape[1]
    units = wg.shape[1]
    half = width // HALVES
    rows = half // LANES
    padded = send1.shape[3] // nodes
    count = nodes * locals_
    depth = HALVES * padded
    peers = [(j, side) for j in range(chips) for side in range(2) if (j, side) != (0, 0)]

    def ahead(j, side):
        return (node, ((chip + j) % chips) * 2 + (core if side == 0 else 1 - core))

    def back(j, side):
        return (node, ((chip + chips - j) % chips) * 2 + (core if side == 0 else 1 - core))

    def load(which, i, p):
        src, dst = ((wg_hbm, wg), (wu_hbm, wu), (wd_hbm, wd))[which]
        if which == 2:
            step = TILE // PIECES
            at = (pl.ds(pl.multiple_of(i * TILE + p * step, step), step), slice(None))
        else:
            step = width // PIECES
            at = (pl.ds(p * step, step), pl.ds(pl.multiple_of(i * TILE, TILE), TILE))
        return pltpu.make_async_copy(src.at[(0, *at)], dst.at[at], w_sem.at[which, i, p])

    def await_load(which, i):
        for p in range(PIECES):
            load(which, i, p).wait()

    barrier = pltpu.get_barrier_semaphore()
    for k in range(1, nodes):
        pl.semaphore_signal(
            barrier, inc=1, device_id=((node + k) % nodes, me), device_id_type=MESH
        )
    for j, side in peers:
        pl.semaphore_signal(barrier, inc=1, device_id=ahead(j, side), device_id_type=MESH)
    for group in ((0, 1), (2,)):
        for i in range(units // TILE):
            for which in group:
                for p in range(PIECES):
                    load(which, i, p).start()

    experts = prob_ref.shape[1]
    for ref, gath in ((tok_ref, gath_x), (dy_ref, gath_dy)):
        stage[...] = jnp.zeros_like(stage)
        for h in range(HALVES):
            for c in range(rows):
                lane, at = h * half + c * LANES, h * padded + c
                stage[at : at + 1, :] = ref[:, lane : lane + LANES].astype(f32)
        if ref is tok_ref:
            stage[rows : rows + 1, 0:experts] = prob_ref[...].astype(f32)
            stage[rows + 1 : rows + 2, 0:experts] = dest_ref[...].astype(f32)
        gath[0, 0, 0] = stage[...].astype(bf16)
    pl.semaphore_wait(barrier, nodes - 1 + len(peers))

    sent = []

    def remote(src, dst, s_sem, r_sem, to):
        return pltpu.make_async_remote_copy(
            src_ref=src,
            dst_ref=dst,
            send_sem=s_sem,
            recv_sem=r_sem,
            device_id=to,
            device_id_type=MESH,
        )

    def send(src, dst, s_sem, r_sem, to):
        copy = remote(src, dst, s_sem, r_sem, to)
        copy.start()
        sent.append(copy)

    def await_recv(ref, s_sem, r_sem):
        remote(ref, ref, s_sem, r_sem, ahead(0, 1)).wait_recv()

    def across(k):
        for j in range(1, chips):
            send(gath_x.at[0, 0, k], gath_x.at[j, 0, k], cs.at[j, k], cr.at[j, k], ahead(j, 0))

    def sideways(j):
        send(gath_x.at[j, 0], gath_x.at[j, 1], ks.at[j], kr.at[j], ahead(0, 1))

    for at, gath in enumerate((gath_x, gath_dy)):
        for k in range(1, nodes):
            to = ((node + k) % nodes, me)
            send(gath.at[0, 0, 0], gath.at[0, 0, k], zs.at[at, k], zr.at[at, k], to)
        if at == 0:
            across(0)
    for k in range(1, nodes):
        await_recv(gath_x.at[0, 0, k], zs.at[0, 0], zr.at[0, k])
        across(k)
    sideways(0)
    for k in range(1, nodes):
        await_recv(gath_dy.at[0, 0, k], zs.at[0, 0], zr.at[1, k])
    for j, side in peers:
        send(
            gath_dy.at[0, 0],
            gath_dy.at[j, side],
            ds.at[j, side],
            dr.at[j, side],
            ahead(j, side),
        )
    for j in range(1, chips):
        for k in range(nodes):
            await_recv(gath_x.at[j, 0, k], cs.at[0, 0], cr.at[j, k])
        sideways(j)
    for j in range(chips):
        await_recv(gath_x.at[j, 1], ks.at[0], kr.at[j])

    def to_rows(gath):
        def widen(l, _):
            block = gath[l // 2, l % 2].astype(f32).reshape(nodes * depth, LANES)
            at = pl.multiple_of(l * (nodes * depth), nodes * depth)
            wide[pl.ds(at, nodes * depth), :] = block
            return 0

        lax.fori_loop(0, locals_, widen, 0)
        for h in range(HALVES):
            for c in range(rows):
                lane, first = h * half + c * LANES, h * padded + c
                rows_ref[:, lane : lane + LANES] = wide[
                    pl.ds(first, count, stride=depth), :
                ].astype(bf16)

    to_rows(gath_x)
    lane_id = lax.broadcasted_iota(jnp.int32, (count, LANES), 1)
    mine = lane_id == me
    probs = wide[pl.ds(rows, count, stride=depth), :]
    dests = wide[pl.ds(rows + 1, count, stride=depth), :]
    prob = jnp.sum(jnp.where(mine, probs, 0.0), axis=1, keepdims=True)
    dest = jnp.sum(jnp.where(mine, dests, 0.0), axis=1, keepdims=True)
    here = dest == node.astype(f32)
    prob = jnp.where(here, prob, 0.0)

    def forward_tile(i, _):
        await_load(0, i)
        await_load(1, i)
        at = pl.ds(pl.multiple_of(i * TILE, TILE), TILE)
        pre_g[:, at] = jnp.dot(rows_ref[...], wg[:, at], preferred_element_type=f32)
        pre_u[:, at] = jnp.dot(rows_ref[...], wu[:, at], preferred_element_type=f32)
        return 0

    lax.fori_loop(0, units // TILE, forward_tile, 0)

    for j, side in peers:
        await_recv(gath_dy.at[j, side], ds.at[0, 0], dr.at[j, side])
    to_rows(gath_dy)

    def hidden_tile(i, gate_sum):
        await_load(2, i)
        at = pl.ds(pl.multiple_of(i * TILE, TILE), TILE)
        pre_gate, pre_up = pre_g[:, at], pre_u[:, at]
        back_hidden = dot_nt(rows_ref[...], wd[at, :])
        logistic = jax.nn.sigmoid(pre_gate)
        swished = pre_gate * logistic
        gate_sum = gate_sum + jnp.sum(swished * pre_up * back_hidden, axis=1, keepdims=True)
        scaled = prob * back_hidden
        dg[:, at] = (scaled * pre_up * logistic * (1.0 + pre_gate * (1.0 - logistic))).astype(bf16)
        du[:, at] = (scaled * swished).astype(bf16)
        return gate_sum

    gate_sum = lax.fori_loop(0, units // TILE, hidden_tile, jnp.zeros((count, 1), f32))
    gate_row = jnp.where(mine & here, gate_sum, 0.0)
    gate_high = gate_row.astype(bf16).astype(f32)

    for h in range(HALVES):
        for extra in range(rows, padded):
            value = jnp.zeros((count, LANES), f32)
            if h == 0 and extra == rows:
                value = gate_high
            if h == 0 and extra == rows + 1:
                value = gate_row - gate_high
            terms[pl.ds(extra, count, stride=padded), :] = value

        def input_tile(i, _):
            at = pl.ds(pl.multiple_of(h * half + i * TILE, TILE), TILE)
            block = dot_nt(dg[...], wg[at, :]) + dot_nt(du[...], wu[at, :])
            for c in range(TILE // LANES):
                terms[pl.ds(i * (TILE // LANES) + c, count, stride=padded), :] = block[
                    :, c * LANES : (c + 1) * LANES
                ]
            return 0

        lax.fori_loop(0, half // TILE, input_tile, 0)
        for j in range(chips):
            for side in range(2):
                at = (j * 2 + side) * nodes * padded
                send1[h, j, side] = terms[at : at + nodes * padded, :].astype(bf16)
                if (j, side) != (0, 0):
                    send(
                        send1.at[h, j, side],
                        recv1.at[h, j, side],
                        ls.at[h, j, side],
                        lr.at[h, j, side],
                        back(j, side),
                    )

    for h in range(HALVES):
        total = send1[h, 0, 0].astype(f32)
        for j, side in peers:
            await_recv(recv1.at[h, j, side], ls.at[h, 0, 0], lr.at[h, j, side])
            total = total + recv1[h, j, side].astype(f32)
        for k in range(nodes):
            part[h, k] = total[k * padded : (k + 1) * padded]
        for k in range(1, nodes):
            to = ((node + nodes - k) % nodes, me)
            send(part.at[h, k], recv2.at[h, k], bs.at[h, k], br.at[h, k], to)
    for h in range(HALVES):
        total = part[h, 0]
        for k in range(1, nodes):
            await_recv(recv2.at[h, k], bs.at[h, 0], br.at[h, k])
            total = total + recv2[h, k]
        out_ref[h] = total
    for copy in sent:
        copy.wait_send()


def fused(nodes, locals_, tokens, out_grad, gate_prob, dest_node, w_gate, w_up, w_down):
    f32, bf16 = jnp.float32, jnp.bfloat16
    width, units = w_gate.shape[1:]
    count = nodes * locals_
    chips = locals_ // 2
    padded = padded_rows(width)
    depth = HALVES * padded
    vmem = pl.BlockSpec(memory_space=pltpu.VMEM)
    hbm = pl.BlockSpec(memory_space=pl.ANY)
    dma = pltpu.SemaphoreType.DMA
    total = pl.pallas_call(
        functools.partial(fused_kernel, nodes, locals_),
        out_shape=jax.ShapeDtypeStruct((HALVES, padded, LANES), f32),
        in_specs=[vmem] * 4 + [hbm] * 3,
        out_specs=vmem,
        scratch_shapes=[
            pltpu.VMEM((width, units), bf16),
            pltpu.VMEM((width, units), bf16),
            pltpu.VMEM((units, width), bf16),
            pltpu.VMEM((depth, LANES), f32),
            pltpu.VMEM((chips, 2, nodes, depth, LANES), bf16),
            pltpu.VMEM((chips, 2, nodes, depth, LANES), bf16),
            pltpu.VMEM((count * depth, LANES), f32),
            pltpu.VMEM((count, width), bf16),
            pltpu.VMEM((count, units), f32),
            pltpu.VMEM((count, units), f32),
            pltpu.VMEM((count, units), bf16),
            pltpu.VMEM((count, units), bf16),
            pltpu.VMEM((count * padded, LANES), f32),
            pltpu.VMEM((HALVES, chips, 2, nodes * padded, LANES), bf16),
            pltpu.VMEM((HALVES, chips, 2, nodes * padded, LANES), bf16),
            pltpu.VMEM((HALVES, nodes, padded, LANES), f32),
            pltpu.VMEM((HALVES, nodes, padded, LANES), f32),
            dma((3, units // TILE, PIECES)),
            dma((2, nodes)),
            dma((2, nodes)),
            dma((chips, nodes)),
            dma((chips, nodes)),
            dma((chips,)),
            dma((chips,)),
            dma((chips, 2)),
            dma((chips, 2)),
            dma((HALVES, chips, 2)),
            dma((HALVES, chips, 2)),
            dma((HALVES, nodes)),
            dma((HALVES, nodes)),
        ],
        compiler_params=pltpu.CompilerParams(
            collective_id=0, has_side_effects=True, vmem_limit_bytes=56 << 20
        ),
        cost_estimate=pl.CostEstimate(
            flops=10 * count * width * units,
            bytes_accessed=6 * width * units,
            transcendentals=count * units,
        ),
    )(tokens, out_grad, gate_prob, dest_node, w_gate, w_up, w_down)
    return pl.pallas_call(
        round_kernel,
        out_shape=(
            jax.ShapeDtypeStruct((1, width), bf16),
            jax.ShapeDtypeStruct(gate_prob.shape, f32),
        ),
        in_specs=[vmem],
        out_specs=(vmem, vmem),
    )(total)


def round_kernel(total_ref, out_ref, gate_ref):
    rows = out_ref.shape[1] // HALVES // LANES
    for h in range(HALVES):
        for c in range(rows):
            lane = (h * rows + c) * LANES
            out_ref[:, lane : lane + LANES] = total_ref[h, c : c + 1].astype(jnp.bfloat16)
    gate = total_ref[0, rows : rows + 1] + total_ref[0, rows + 1 : rows + 2]
    gate_ref[...] = gate[:, 0 : gate_ref.shape[1]]


def padded_rows(width):
    return -(-(width // HALVES // LANES + 2) // 16) * 16


def on_device(nodes, locals_, tokens, out_grad, gate_prob, dest_node, w_gate, w_up, w_down):
    width, units = w_gate.shape[1:]
    weights = 6 * width * units
    rows = nodes * locals_ * 2 * HALVES * padded_rows(width) * LANES * 10
    small = (
        tokens.shape[0] == 1
        and gate_prob.shape[1] == locals_
        and locals_ % 2 == 0
        and width % (HALVES * TILE) == 0
        and units % TILE == 0
        and weights + rows < 40 << 20
    )
    plan = functools.partial(fused, nodes, locals_) if small else routed
    return plan(tokens, out_grad, gate_prob, dest_node, w_gate, w_up, w_down)


def solution(mesh):
    split = ("node", "local")
    return jax.shard_map(
        functools.partial(on_device, mesh.shape["node"], mesh.shape["local"]),
        mesh=mesh,
        in_specs=(P(split, None),) * 4 + (P(split, None, None),) * 3,
        out_specs=(P(split, None), P(split, None)),
        check_vma=False,
    )
```

```python
import functools

import jax
import jax.numpy as jnp
from jax import lax
from jax.experimental import pallas as pl
from jax.experimental.pallas import tpu as pltpu
from jax.sharding import PartitionSpec as P

MESH = pl.DeviceIdType.MESH
LANES = 128
TILE = 512
COLUMNS = 256
HALVES = 2
PIECES = 4


def expert_terms(rows_x, rows_dy, rows_gate, weight_gate, weight_up, weight_down):
    contract = (((1,), (1,)), ((), ()))
    pre_gate = jnp.dot(rows_x, weight_gate, preferred_element_type=jnp.float32)
    pre_up = jnp.dot(rows_x, weight_up, preferred_element_type=jnp.float32)
    logistic = jax.nn.sigmoid(pre_gate)
    swished = pre_gate * logistic
    hidden = swished * pre_up
    back_hidden = lax.dot_general(
        rows_dy, weight_down, contract, preferred_element_type=jnp.float32
    )
    gate_terms = jnp.sum(hidden * back_hidden, axis=1)
    scaled = rows_gate[:, None] * back_hidden
    grad_gate = (scaled * pre_up * logistic * (1.0 + pre_gate * (1.0 - logistic))).astype(
        jnp.bfloat16
    )
    grad_up = (scaled * swished).astype(jnp.bfloat16)
    input_terms = lax.dot_general(
        grad_gate, weight_gate, contract, preferred_element_type=jnp.float32
    )
    input_terms = input_terms + lax.dot_general(
        grad_up, weight_up, contract, preferred_element_type=jnp.float32
    )
    return (input_terms, gate_terms)


def routed(tokens, out_grad, gate_prob, dest_node, w_gate, w_up, w_down):
    node_count = lax.axis_size("node")
    local_count = lax.axis_size("local")
    local_id = lax.axis_index("local")
    width = tokens.shape[1]
    experts_here = gate_prob.shape[1]
    shards = local_count // experts_here
    column = local_id // shards
    pick_float = (jnp.arange(experts_here) == column).astype(jnp.float32)
    dest_half = dest_node.astype(jnp.bfloat16)
    home_x, home_dy, home_gate, home_dest = (
        lax.all_gather(tokens, "local", axis=0, tiled=True),
        lax.all_gather(out_grad, "local", axis=0, tiled=True),
        lax.all_gather(gate_prob, "local", axis=0, tiled=True),
        lax.all_gather(dest_half, "local", axis=0, tiled=True),
    )
    members = home_x.shape[0]
    capacity = 2 * members // node_count
    slots = node_count * capacity
    target = jnp.sum(home_dest.astype(jnp.float32) * pick_float[None, :], axis=1).astype(jnp.int32)
    onehot_dest = (target[:, None] == jnp.arange(node_count)[None, :]).astype(jnp.int32)
    before = jnp.cumsum(onehot_dest, axis=0) - onehot_dest
    position = target * capacity + jnp.sum(before * onehot_dest, axis=1)
    place_half = (jnp.arange(slots)[:, None] == position[None, :]).astype(jnp.bfloat16)
    send_x = jnp.dot(place_half, home_x, preferred_element_type=jnp.float32).astype(jnp.bfloat16)
    send_dy = jnp.dot(place_half, home_dy, preferred_element_type=jnp.float32).astype(jnp.bfloat16)
    send_gate = jnp.dot(place_half, home_gate, preferred_element_type=jnp.float32).astype(
        jnp.bfloat16
    )

    def over_node(rows):
        return lax.all_to_all(
            rows.reshape(node_count, -1, rows.shape[1]),
            "node",
            split_axis=0,
            concat_axis=0,
            tiled=True,
        ).reshape(rows.shape)

    part_x, part_dy, part_gate = over_node(send_x), over_node(send_dy), over_node(send_gate)
    rows_gate = jnp.sum(part_gate.astype(jnp.float32) * pick_float[None, :], axis=1)
    input_terms, gate_terms = expert_terms(
        part_x, part_dy, rows_gate, w_gate[0], w_up[0], w_down[0]
    )
    gate_cols = gate_terms[:, None] * pick_float[None, :]
    back_x, back_gate = over_node(input_terms), over_node(gate_cols)
    term_x = jnp.take(back_x, position, axis=0)
    term_gate = jnp.take(back_gate, position, axis=0)
    summed_x, summed_gate = (
        lax.psum_scatter(term_x, "local", scatter_dimension=0, tiled=True),
        lax.psum_scatter(term_gate, "local", scatter_dimension=0, tiled=True),
    )
    return (summed_x.astype(jnp.bfloat16), summed_gate)


def dot_nt(a, b):
    return lax.dot_general(a, b, (((1,), (1,)), ((), ())), preferred_element_type=jnp.float32)


def fused_kernel(
    nodes,
    locals_,
    tok_ref,
    dy_ref,
    prob_ref,
    dest_ref,
    wg_hbm,
    wu_hbm,
    wd_hbm,
    out_ref,
    wg,
    wu,
    wd,
    stage,
    gath_x,
    gath_dy,
    wide,
    rows_ref,
    pre_g,
    pre_u,
    dg,
    du,
    terms,
    send1,
    recv1,
    part,
    recv2,
    w_sem,
    zs,
    zr,
    cs,
    cr,
    ks,
    kr,
    ds,
    dr,
    ls,
    lr,
    bs,
    br,
):
    f32, bf16 = jnp.float32, jnp.bfloat16
    node, me = lax.axis_index("node"), lax.axis_index("local")
    chips = locals_ // 2
    chip, core = me // 2, me % 2
    width = tok_ref.shape[1]
    units = wg.shape[1]
    half = width // HALVES
    rows = half // LANES
    padded = send1.shape[3] // nodes
    count = nodes * locals_
    depth = HALVES * padded
    peers = [(j, side) for j in range(chips) for side in range(2) if (j, side) != (0, 0)]

    def ahead(j, side):
        return (node, ((chip + j) % chips) * 2 + (core if side == 0 else 1 - core))

    def back(j, side):
        return (node, ((chip + chips - j) % chips) * 2 + (core if side == 0 else 1 - core))

    def load(which, i, p):
        src, dst = ((wg_hbm, wg), (wu_hbm, wu), (wd_hbm, wd))[which]
        if which == 2:
            step = TILE // PIECES
            at = (pl.ds(i * TILE + p * step, step), slice(None))
        else:
            step = width // PIECES
            at = (pl.ds(p * step, step), pl.ds(i * TILE, TILE))
        return pltpu.make_async_copy(src.at[(0, *at)], dst.at[at], w_sem.at[which, i, p])

    def await_load(which, i):
        for p in range(PIECES):
            load(which, i, p).wait()

    waiting = [
        (which, i, p)
        for group in ((0, 1), (2,))
        for i in range(units // TILE)
        for which in group
        for p in range(PIECES)
    ]

    def issue(number):
        for _ in range(min(number, len(waiting))):
            load(*waiting.pop(0)).start()

    barrier = pltpu.get_barrier_semaphore()
    for k in range(1, nodes):
        pl.semaphore_signal(
            barrier, inc=1, device_id=((node + k) % nodes, me), device_id_type=MESH
        )
    for j, side in peers:
        pl.semaphore_signal(barrier, inc=1, device_id=ahead(j, side), device_id_type=MESH)
    issue(4)

    experts = prob_ref.shape[1]
    for ref, gath in ((tok_ref, gath_x), (dy_ref, gath_dy)):
        stage[...] = jnp.zeros_like(stage)
        for h in range(HALVES):
            for c in range(rows):
                lane, at = h * half + c * LANES, h * padded + c
                stage[at : at + 1, :] = ref[:, lane : lane + LANES].astype(f32)
        if ref is tok_ref:
            stage[rows : rows + 1, 0:experts] = prob_ref[...].astype(f32)
            stage[rows + 1 : rows + 2, 0:experts] = dest_ref[...].astype(f32)
        gath[0, 0, 0] = stage[...].astype(bf16)
    pl.semaphore_wait(barrier, nodes - 1 + len(peers))

    sent = []

    def remote(src, dst, s_sem, r_sem, to):
        return pltpu.make_async_remote_copy(
            src_ref=src,
            dst_ref=dst,
            send_sem=s_sem,
            recv_sem=r_sem,
            device_id=to,
            device_id_type=MESH,
        )

    def send(src, dst, s_sem, r_sem, to):
        copy = remote(src, dst, s_sem, r_sem, to)
        copy.start()
        sent.append(copy)

    def await_recv(ref, s_sem, r_sem):
        remote(ref, ref, s_sem, r_sem, ahead(0, 1)).wait_recv()

    def across(k):
        for j in range(1, chips):
            send(gath_x.at[0, 0, k], gath_x.at[j, 0, k], cs.at[j, k], cr.at[j, k], ahead(j, 0))

    def sideways(j):
        send(gath_x.at[j, 0], gath_x.at[j, 1], ks.at[j], kr.at[j], ahead(0, 1))

    for at, gath in enumerate((gath_x, gath_dy)):
        for k in range(1, nodes):
            to = ((node + k) % nodes, me)
            send(gath.at[0, 0, 0], gath.at[0, 0, k], zs.at[at, k], zr.at[at, k], to)
        if at == 0:
            across(0)
    issue(3)
    for k in range(1, nodes):
        await_recv(gath_x.at[0, 0, k], zs.at[0, 0], zr.at[0, k])
        across(k)
        issue(1)
    sideways(0)
    issue(1)
    for k in range(1, nodes):
        await_recv(gath_dy.at[0, 0, k], zs.at[0, 0], zr.at[1, k])
    for j, side in peers:
        send(
            gath_dy.at[0, 0],
            gath_dy.at[j, side],
            ds.at[j, side],
            dr.at[j, side],
            ahead(j, side),
        )
    issue(2)
    for j in range(1, chips):
        for k in range(nodes):
            await_recv(gath_x.at[j, 0, k], cs.at[0, 0], cr.at[j, k])
        sideways(j)
        issue(1)
    issue(len(waiting))
    for j in range(chips):
        await_recv(gath_x.at[j, 1], ks.at[0], kr.at[j])

    def to_rows(gath):
        def widen(l, _):
            block = gath[l // 2, l % 2].astype(f32).reshape(nodes * depth, LANES)
            at = pl.multiple_of(l * (nodes * depth), nodes * depth)
            wide[pl.ds(at, nodes * depth), :] = block
            return 0

        lax.fori_loop(0, locals_, widen, 0)
        for h in range(HALVES):
            for c in range(rows):
                lane, first = h * half + c * LANES, h * padded + c
                rows_ref[:, lane : lane + LANES] = wide[
                    pl.ds(first, count, stride=depth), :
                ].astype(bf16)

    to_rows(gath_x)
    lane_id = lax.broadcasted_iota(jnp.int32, (count, LANES), 1)
    mine = lane_id == me
    probs = wide[pl.ds(rows, count, stride=depth), :]
    dests = wide[pl.ds(rows + 1, count, stride=depth), :]
    prob = jnp.sum(jnp.where(mine, probs, 0.0), axis=1, keepdims=True)
    dest = jnp.sum(jnp.where(mine, dests, 0.0), axis=1, keepdims=True)
    here = dest == node.astype(f32)
    prob = jnp.where(here, prob, 0.0)

    for i in range(units // TILE):
        await_load(0, i)
        await_load(1, i)
        at = pl.ds(i * TILE, TILE)
        pre_g[:, at] = jnp.dot(rows_ref[...], wg[:, at], preferred_element_type=f32)
        pre_u[:, at] = jnp.dot(rows_ref[...], wu[:, at], preferred_element_type=f32)

    for j, side in peers:
        await_recv(gath_dy.at[j, side], ds.at[0, 0], dr.at[j, side])
    to_rows(gath_dy)

    gate_sum = jnp.zeros((count, 1), f32)
    for i in range(units // TILE):
        await_load(2, i)
        at = pl.ds(i * TILE, TILE)
        pre_gate, pre_up = pre_g[:, at], pre_u[:, at]
        back_hidden = dot_nt(rows_ref[...], wd[at, :])
        logistic = jax.nn.sigmoid(pre_gate)
        swished = pre_gate * logistic
        gate_sum = gate_sum + jnp.sum(swished * pre_up * back_hidden, axis=1, keepdims=True)
        scaled = prob * back_hidden
        dg[:, at] = (scaled * pre_up * logistic * (1.0 + pre_gate * (1.0 - logistic))).astype(bf16)
        du[:, at] = (scaled * swished).astype(bf16)
    gate_row = jnp.where(mine & here, gate_sum, 0.0)
    gate_high = gate_row.astype(bf16).astype(f32)

    for h in range(HALVES):
        for extra in range(rows, padded):
            value = jnp.zeros((count, LANES), f32)
            if h == 0 and extra == rows:
                value = gate_high
            if h == 0 and extra == rows + 1:
                value = gate_row - gate_high
            terms[pl.ds(extra, count, stride=padded), :] = value

        for i in range(half // COLUMNS):
            at = pl.ds(h * half + i * COLUMNS, COLUMNS)
            block = dot_nt(dg[...], wg[at, :]) + dot_nt(du[...], wu[at, :])
            for c in range(COLUMNS // LANES):
                terms[pl.ds(i * (COLUMNS // LANES) + c, count, stride=padded), :] = block[
                    :, c * LANES : (c + 1) * LANES
                ]
        for j in range(chips):
            for side in range(2):
                at = (j * 2 + side) * nodes * padded
                send1[h, j, side] = terms[at : at + nodes * padded, :].astype(bf16)
                if (j, side) != (0, 0):
                    send(
                        send1.at[h, j, side],
                        recv1.at[h, j, side],
                        ls.at[h, j, side],
                        lr.at[h, j, side],
                        back(j, side),
                    )

    for h in range(HALVES):
        total = send1[h, 0, 0].astype(f32)
        for j, side in peers:
            await_recv(recv1.at[h, j, side], ls.at[h, 0, 0], lr.at[h, j, side])
            total = total + recv1[h, j, side].astype(f32)
        for k in range(nodes):
            part[h, k] = total[k * padded : (k + 1) * padded]
        for k in range(1, nodes):
            to = ((node + nodes - k) % nodes, me)
            send(part.at[h, k], recv2.at[h, k], bs.at[h, k], br.at[h, k], to)
    for h in range(HALVES):
        total = part[h, 0]
        for k in range(1, nodes):
            await_recv(recv2.at[h, k], bs.at[h, 0], br.at[h, k])
            total = total + recv2[h, k]
        out_ref[h] = total
    for copy in sent:
        copy.wait_send()


def fused(nodes, locals_, tokens, out_grad, gate_prob, dest_node, w_gate, w_up, w_down):
    f32, bf16 = jnp.float32, jnp.bfloat16
    width, units = w_gate.shape[1:]
    count = nodes * locals_
    chips = locals_ // 2
    padded = padded_rows(width)
    depth = HALVES * padded
    vmem = pl.BlockSpec(memory_space=pltpu.VMEM)
    hbm = pl.BlockSpec(memory_space=pl.ANY)
    dma = pltpu.SemaphoreType.DMA
    total = pl.pallas_call(
        functools.partial(fused_kernel, nodes, locals_),
        out_shape=jax.ShapeDtypeStruct((HALVES, padded, LANES), f32),
        in_specs=[vmem] * 4 + [hbm] * 3,
        out_specs=vmem,
        scratch_shapes=[
            pltpu.VMEM((width, units), bf16),
            pltpu.VMEM((width, units), bf16),
            pltpu.VMEM((units, width), bf16),
            pltpu.VMEM((depth, LANES), f32),
            pltpu.VMEM((chips, 2, nodes, depth, LANES), bf16),
            pltpu.VMEM((chips, 2, nodes, depth, LANES), bf16),
            pltpu.VMEM((count * depth, LANES), f32),
            pltpu.VMEM((count, width), bf16),
            pltpu.VMEM((count, units), f32),
            pltpu.VMEM((count, units), f32),
            pltpu.VMEM((count, units), bf16),
            pltpu.VMEM((count, units), bf16),
            pltpu.VMEM((count * padded, LANES), f32),
            pltpu.VMEM((HALVES, chips, 2, nodes * padded, LANES), bf16),
            pltpu.VMEM((HALVES, chips, 2, nodes * padded, LANES), bf16),
            pltpu.VMEM((HALVES, nodes, padded, LANES), f32),
            pltpu.VMEM((HALVES, nodes, padded, LANES), f32),
            dma((3, units // TILE, PIECES)),
            dma((2, nodes)),
            dma((2, nodes)),
            dma((chips, nodes)),
            dma((chips, nodes)),
            dma((chips,)),
            dma((chips,)),
            dma((chips, 2)),
            dma((chips, 2)),
            dma((HALVES, chips, 2)),
            dma((HALVES, chips, 2)),
            dma((HALVES, nodes)),
            dma((HALVES, nodes)),
        ],
        compiler_params=pltpu.CompilerParams(
            collective_id=0, has_side_effects=True, vmem_limit_bytes=56 << 20
        ),
        cost_estimate=pl.CostEstimate(
            flops=10 * count * width * units,
            bytes_accessed=6 * width * units,
            transcendentals=count * units,
        ),
    )(tokens, out_grad, gate_prob, dest_node, w_gate, w_up, w_down)
    return pl.pallas_call(
        round_kernel,
        out_shape=(
            jax.ShapeDtypeStruct((1, width), bf16),
            jax.ShapeDtypeStruct(gate_prob.shape, f32),
        ),
        in_specs=[vmem],
        out_specs=(vmem, vmem),
    )(total)


def round_kernel(total_ref, out_ref, gate_ref):
    rows = out_ref.shape[1] // HALVES // LANES
    for h in range(HALVES):
        for c in range(rows):
            lane = (h * rows + c) * LANES
            out_ref[:, lane : lane + LANES] = total_ref[h, c : c + 1].astype(jnp.bfloat16)
    gate = total_ref[0, rows : rows + 1] + total_ref[0, rows + 1 : rows + 2]
    gate_ref[...] = gate[:, 0 : gate_ref.shape[1]]


def padded_rows(width):
    return -(-(width // HALVES // LANES + 2) // 16) * 16


def on_device(nodes, locals_, tokens, out_grad, gate_prob, dest_node, w_gate, w_up, w_down):
    width, units = w_gate.shape[1:]
    weights = 6 * width * units
    rows = nodes * locals_ * 2 * HALVES * padded_rows(width) * LANES * 10
    small = (
        tokens.shape[0] == 1
        and gate_prob.shape[1] == locals_
        and locals_ % 2 == 0
        and width % (HALVES * COLUMNS) == 0
        and width % (16 * PIECES) == 0
        and units % TILE == 0
        and weights + rows < 40 << 20
    )
    plan = functools.partial(fused, nodes, locals_) if small else routed
    return plan(tokens, out_grad, gate_prob, dest_node, w_gate, w_up, w_down)


def solution(mesh):
    split = ("node", "local")
    return jax.shard_map(
        functools.partial(on_device, mesh.shape["node"], mesh.shape["local"]),
        mesh=mesh,
        in_specs=(P(split, None),) * 4 + (P(split, None, None),) * 3,
        out_specs=(P(split, None), P(split, None)),
        check_vma=False,
    )
```

```python
import functools

import jax
import jax.numpy as jnp
from jax import lax
from jax.experimental import pallas as pl
from jax.experimental.pallas import tpu as pltpu
from jax.sharding import PartitionSpec as P

MESH = pl.DeviceIdType.MESH
LANES = 128
TILE = 512
COLUMNS = 256
HALVES = 2
PIECES = 4


def expert_terms(rows_x, rows_dy, rows_gate, weight_gate, weight_up, weight_down):
    contract = (((1,), (1,)), ((), ()))
    pre_gate = jnp.dot(rows_x, weight_gate, preferred_element_type=jnp.float32)
    pre_up = jnp.dot(rows_x, weight_up, preferred_element_type=jnp.float32)
    logistic = jax.nn.sigmoid(pre_gate)
    swished = pre_gate * logistic
    hidden = swished * pre_up
    back_hidden = lax.dot_general(
        rows_dy, weight_down, contract, preferred_element_type=jnp.float32
    )
    gate_terms = jnp.sum(hidden * back_hidden, axis=1)
    scaled = rows_gate[:, None] * back_hidden
    grad_gate = (scaled * pre_up * logistic * (1.0 + pre_gate * (1.0 - logistic))).astype(
        jnp.bfloat16
    )
    grad_up = (scaled * swished).astype(jnp.bfloat16)
    input_terms = lax.dot_general(
        grad_gate, weight_gate, contract, preferred_element_type=jnp.float32
    )
    input_terms = input_terms + lax.dot_general(
        grad_up, weight_up, contract, preferred_element_type=jnp.float32
    )
    return (input_terms, gate_terms)


def routed(tokens, out_grad, gate_prob, dest_node, w_gate, w_up, w_down):
    node_count = lax.axis_size("node")
    local_count = lax.axis_size("local")
    local_id = lax.axis_index("local")
    width = tokens.shape[1]
    experts_here = gate_prob.shape[1]
    shards = local_count // experts_here
    column = local_id // shards
    pick_float = (jnp.arange(experts_here) == column).astype(jnp.float32)
    dest_half = dest_node.astype(jnp.bfloat16)
    home_x, home_dy, home_gate, home_dest = (
        lax.all_gather(tokens, "local", axis=0, tiled=True),
        lax.all_gather(out_grad, "local", axis=0, tiled=True),
        lax.all_gather(gate_prob, "local", axis=0, tiled=True),
        lax.all_gather(dest_half, "local", axis=0, tiled=True),
    )
    members = home_x.shape[0]
    capacity = 2 * members // node_count
    slots = node_count * capacity
    target = jnp.sum(home_dest.astype(jnp.float32) * pick_float[None, :], axis=1).astype(jnp.int32)
    onehot_dest = (target[:, None] == jnp.arange(node_count)[None, :]).astype(jnp.int32)
    before = jnp.cumsum(onehot_dest, axis=0) - onehot_dest
    position = target * capacity + jnp.sum(before * onehot_dest, axis=1)
    place_half = (jnp.arange(slots)[:, None] == position[None, :]).astype(jnp.bfloat16)
    send_x = jnp.dot(place_half, home_x, preferred_element_type=jnp.float32).astype(jnp.bfloat16)
    send_dy = jnp.dot(place_half, home_dy, preferred_element_type=jnp.float32).astype(jnp.bfloat16)
    send_gate = jnp.dot(place_half, home_gate, preferred_element_type=jnp.float32).astype(
        jnp.bfloat16
    )

    def over_node(rows):
        return lax.all_to_all(
            rows.reshape(node_count, -1, rows.shape[1]),
            "node",
            split_axis=0,
            concat_axis=0,
            tiled=True,
        ).reshape(rows.shape)

    part_x, part_dy, part_gate = over_node(send_x), over_node(send_dy), over_node(send_gate)
    rows_gate = jnp.sum(part_gate.astype(jnp.float32) * pick_float[None, :], axis=1)
    input_terms, gate_terms = expert_terms(
        part_x, part_dy, rows_gate, w_gate[0], w_up[0], w_down[0]
    )
    gate_cols = gate_terms[:, None] * pick_float[None, :]
    back_x, back_gate = over_node(input_terms), over_node(gate_cols)
    term_x = jnp.take(back_x, position, axis=0)
    term_gate = jnp.take(back_gate, position, axis=0)
    summed_x, summed_gate = (
        lax.psum_scatter(term_x, "local", scatter_dimension=0, tiled=True),
        lax.psum_scatter(term_gate, "local", scatter_dimension=0, tiled=True),
    )
    return (summed_x.astype(jnp.bfloat16), summed_gate)


def dot_nt(a, b):
    return lax.dot_general(a, b, (((1,), (1,)), ((), ())), preferred_element_type=jnp.float32)


def fused_kernel(
    nodes,
    locals_,
    tok_ref,
    dy_ref,
    prob_ref,
    dest_ref,
    wg_hbm,
    wu_hbm,
    wd_hbm,
    out_ref,
    wg,
    wu,
    wd,
    stage,
    gath_x,
    gath_dy,
    wide,
    rows_ref,
    pre_g,
    pre_u,
    dg,
    du,
    terms,
    send1,
    recv1,
    part,
    recv2,
    w_sem,
    zs,
    zr,
    cs,
    cr,
    ks,
    kr,
    ds,
    dr,
    ls,
    lr,
    bs,
    br,
):
    f32, bf16 = jnp.float32, jnp.bfloat16
    node, me = lax.axis_index("node"), lax.axis_index("local")
    chips = locals_ // 2
    chip, core = me // 2, me % 2
    width = tok_ref.shape[1]
    units = wg.shape[1]
    half = width // HALVES
    rows = half // LANES
    padded = send1.shape[3] // nodes
    count = nodes * locals_
    depth = HALVES * padded
    peers = [(j, side) for j in range(chips) for side in range(2) if (j, side) != (0, 0)]

    def ahead(j, side):
        return (node, ((chip + j) % chips) * 2 + (core if side == 0 else 1 - core))

    def back(j, side):
        return (node, ((chip + chips - j) % chips) * 2 + (core if side == 0 else 1 - core))

    def load(which, i, p):
        src, dst = ((wg_hbm, wg), (wu_hbm, wu), (wd_hbm, wd))[which]
        if which == 2:
            step = TILE // PIECES
            at = (pl.ds(i * TILE + p * step, step), slice(None))
        else:
            step = width // PIECES
            at = (pl.ds(p * step, step), pl.ds(i * TILE, TILE))
        return pltpu.make_async_copy(src.at[(0, *at)], dst.at[at], w_sem.at[which, i, p])

    def await_load(which, i):
        for p in range(PIECES):
            load(which, i, p).wait()

    pieces = [
        (which, i, p)
        for group in ((0, 1), (2,))
        for i in range(units // TILE)
        for which in group
        for p in range(PIECES)
    ]

    barrier = pltpu.get_barrier_semaphore()
    for k in range(1, nodes):
        pl.semaphore_signal(
            barrier, inc=1, device_id=((node + k) % nodes, me), device_id_type=MESH
        )
    for j, side in peers:
        pl.semaphore_signal(barrier, inc=1, device_id=ahead(j, side), device_id_type=MESH)
    for piece in pieces:
        load(*piece).start()

    experts = prob_ref.shape[1]
    for ref, gath in ((tok_ref, gath_x), (dy_ref, gath_dy)):
        stage[...] = jnp.zeros_like(stage)
        for h in range(HALVES):
            for c in range(rows):
                lane, at = h * half + c * LANES, h * padded + c
                stage[at : at + 1, :] = ref[:, lane : lane + LANES].astype(f32)
        if ref is tok_ref:
            stage[rows : rows + 1, 0:experts] = prob_ref[...].astype(f32)
            stage[rows + 1 : rows + 2, 0:experts] = dest_ref[...].astype(f32)
        gath[0, 0, 0] = stage[...].astype(bf16)
    pl.semaphore_wait(barrier, nodes - 1 + len(peers))

    sent = []

    def remote(src, dst, s_sem, r_sem, to):
        return pltpu.make_async_remote_copy(
            src_ref=src,
            dst_ref=dst,
            send_sem=s_sem,
            recv_sem=r_sem,
            device_id=to,
            device_id_type=MESH,
        )

    def send(src, dst, s_sem, r_sem, to):
        copy = remote(src, dst, s_sem, r_sem, to)
        copy.start()
        sent.append(copy)

    def await_recv(ref, s_sem, r_sem):
        remote(ref, ref, s_sem, r_sem, ahead(0, 1)).wait_recv()

    def across(k):
        for j in range(1, chips):
            send(gath_x.at[0, 0, k], gath_x.at[j, 0, k], cs.at[j, k], cr.at[j, k], ahead(j, 0))

    def sideways(j):
        send(gath_x.at[j, 0], gath_x.at[j, 1], ks.at[j], kr.at[j], ahead(0, 1))

    for at, gath in enumerate((gath_x, gath_dy)):
        for k in range(1, nodes):
            to = ((node + k) % nodes, me)
            send(gath.at[0, 0, 0], gath.at[0, 0, k], zs.at[at, k], zr.at[at, k], to)
        if at == 0:
            across(0)
    for k in range(1, nodes):
        await_recv(gath_x.at[0, 0, k], zs.at[0, 0], zr.at[0, k])
        across(k)
    sideways(0)
    for k in range(1, nodes):
        await_recv(gath_dy.at[0, 0, k], zs.at[0, 0], zr.at[1, k])
    for j, side in peers:
        send(
            gath_dy.at[0, 0],
            gath_dy.at[j, side],
            ds.at[j, side],
            dr.at[j, side],
            ahead(j, side),
        )
    for j in range(1, chips):
        for k in range(nodes):
            await_recv(gath_x.at[j, 0, k], cs.at[0, 0], cr.at[j, k])
        sideways(j)
    for j in range(chips):
        await_recv(gath_x.at[j, 1], ks.at[0], kr.at[j])

    def to_rows(gath):
        def widen(l, _):
            block = gath[l // 2, l % 2].astype(f32).reshape(nodes * depth, LANES)
            at = pl.multiple_of(l * (nodes * depth), nodes * depth)
            wide[pl.ds(at, nodes * depth), :] = block
            return 0

        lax.fori_loop(0, locals_, widen, 0)
        for h in range(HALVES):
            for c in range(rows):
                lane, first = h * half + c * LANES, h * padded + c
                rows_ref[:, lane : lane + LANES] = wide[
                    pl.ds(first, count, stride=depth), :
                ].astype(bf16)

    to_rows(gath_x)
    lane_id = lax.broadcasted_iota(jnp.int32, (count, LANES), 1)
    mine = lane_id == me
    probs = wide[pl.ds(rows, count, stride=depth), :]
    dests = wide[pl.ds(rows + 1, count, stride=depth), :]
    prob = jnp.sum(jnp.where(mine, probs, 0.0), axis=1, keepdims=True)
    dest = jnp.sum(jnp.where(mine, dests, 0.0), axis=1, keepdims=True)
    here = dest == node.astype(f32)
    prob = jnp.where(here, prob, 0.0)

    for i in range(units // TILE):
        await_load(0, i)
        await_load(1, i)
        at = pl.ds(i * TILE, TILE)
        pre_g[:, at] = jnp.dot(rows_ref[...], wg[:, at], preferred_element_type=f32)
        pre_u[:, at] = jnp.dot(rows_ref[...], wu[:, at], preferred_element_type=f32)

    for j, side in peers:
        await_recv(gath_dy.at[j, side], ds.at[0, 0], dr.at[j, side])
    to_rows(gath_dy)

    gate_sum = jnp.zeros((count, 1), f32)
    for i in range(units // TILE):
        await_load(2, i)
        at = pl.ds(i * TILE, TILE)
        pre_gate, pre_up = pre_g[:, at], pre_u[:, at]
        back_hidden = dot_nt(rows_ref[...], wd[at, :])
        logistic = jax.nn.sigmoid(pre_gate)
        swished = pre_gate * logistic
        gate_sum = gate_sum + jnp.sum(swished * pre_up * back_hidden, axis=1, keepdims=True)
        scaled = prob * back_hidden
        dg[:, at] = (scaled * pre_up * logistic * (1.0 + pre_gate * (1.0 - logistic))).astype(bf16)
        du[:, at] = (scaled * swished).astype(bf16)
    gate_row = jnp.where(mine & here, gate_sum, 0.0)
    gate_high = gate_row.astype(bf16).astype(f32)

    for h in range(HALVES):
        for extra in range(rows, padded):
            value = jnp.zeros((count, LANES), f32)
            if h == 0 and extra == rows:
                value = gate_high
            if h == 0 and extra == rows + 1:
                value = gate_row - gate_high
            terms[pl.ds(extra, count, stride=padded), :] = value

        for i in range(half // COLUMNS):
            at = pl.ds(h * half + i * COLUMNS, COLUMNS)
            block = dot_nt(dg[...], wg[at, :]) + dot_nt(du[...], wu[at, :])
            for c in range(COLUMNS // LANES):
                terms[pl.ds(i * (COLUMNS // LANES) + c, count, stride=padded), :] = block[
                    :, c * LANES : (c + 1) * LANES
                ]
        for j in range(chips):
            for side in range(2):
                at = (j * 2 + side) * nodes * padded
                send1[h, j, side] = terms[at : at + nodes * padded, :].astype(bf16)
                if (j, side) != (0, 0):
                    send(
                        send1.at[h, j, side],
                        recv1.at[h, j, side],
                        ls.at[h, j, side],
                        lr.at[h, j, side],
                        back(j, side),
                    )

    def drain():
        while sent:
            sent.pop(0).wait_send()

    drain()
    for h in range(HALVES):
        total = send1[h, 0, 0].astype(f32)
        for j, side in peers:
            await_recv(recv1.at[h, j, side], ls.at[h, 0, 0], lr.at[h, j, side])
            total = total + recv1[h, j, side].astype(f32)
        for k in range(nodes):
            part[h, k] = total[k * padded : (k + 1) * padded]
        for k in range(1, nodes):
            to = ((node + nodes - k) % nodes, me)
            send(part.at[h, k], recv2.at[h, k], bs.at[h, k], br.at[h, k], to)
    for h in range(HALVES):
        total = part[h, 0]
        for k in range(1, nodes):
            await_recv(recv2.at[h, k], bs.at[h, 0], br.at[h, k])
            total = total + recv2[h, k]
        out_ref[h] = total
    drain()


def fused(nodes, locals_, tokens, out_grad, gate_prob, dest_node, w_gate, w_up, w_down):
    f32, bf16 = jnp.float32, jnp.bfloat16
    width, units = w_gate.shape[1:]
    count = nodes * locals_
    chips = locals_ // 2
    padded = padded_rows(width)
    depth = HALVES * padded
    vmem = pl.BlockSpec(memory_space=pltpu.VMEM)
    hbm = pl.BlockSpec(memory_space=pl.ANY)
    dma = pltpu.SemaphoreType.DMA
    total = pl.pallas_call(
        functools.partial(fused_kernel, nodes, locals_),
        out_shape=jax.ShapeDtypeStruct((HALVES, padded, LANES), f32),
        in_specs=[vmem] * 4 + [hbm] * 3,
        out_specs=vmem,
        scratch_shapes=[
            pltpu.VMEM((width, units), bf16),
            pltpu.VMEM((width, units), bf16),
            pltpu.VMEM((units, width), bf16),
            pltpu.VMEM((depth, LANES), f32),
            pltpu.VMEM((chips, 2, nodes, depth, LANES), bf16),
            pltpu.VMEM((chips, 2, nodes, depth, LANES), bf16),
            pltpu.VMEM((count * depth, LANES), f32),
            pltpu.VMEM((count, width), bf16),
            pltpu.VMEM((count, units), f32),
            pltpu.VMEM((count, units), f32),
            pltpu.VMEM((count, units), bf16),
            pltpu.VMEM((count, units), bf16),
            pltpu.VMEM((count * padded, LANES), f32),
            pltpu.VMEM((HALVES, chips, 2, nodes * padded, LANES), bf16),
            pltpu.VMEM((HALVES, chips, 2, nodes * padded, LANES), bf16),
            pltpu.VMEM((HALVES, nodes, padded, LANES), f32),
            pltpu.VMEM((HALVES, nodes, padded, LANES), f32),
            dma((3, units // TILE, PIECES)),
            dma((2, nodes)),
            dma((2, nodes)),
            dma((chips, nodes)),
            dma((chips, nodes)),
            dma((chips,)),
            dma((chips,)),
            dma((chips, 2)),
            dma((chips, 2)),
            dma((HALVES, chips, 2)),
            dma((HALVES, chips, 2)),
            dma((HALVES, nodes)),
            dma((HALVES, nodes)),
        ],
        compiler_params=pltpu.CompilerParams(
            collective_id=0, has_side_effects=True, vmem_limit_bytes=56 << 20
        ),
        cost_estimate=pl.CostEstimate(
            flops=10 * count * width * units,
            bytes_accessed=6 * width * units,
            transcendentals=count * units,
        ),
    )(tokens, out_grad, gate_prob, dest_node, w_gate, w_up, w_down)
    return pl.pallas_call(
        round_kernel,
        out_shape=(
            jax.ShapeDtypeStruct((1, width), bf16),
            jax.ShapeDtypeStruct(gate_prob.shape, f32),
        ),
        in_specs=[vmem],
        out_specs=(vmem, vmem),
    )(total)


def round_kernel(total_ref, out_ref, gate_ref):
    rows = out_ref.shape[1] // HALVES // LANES
    for h in range(HALVES):
        for c in range(rows):
            lane = (h * rows + c) * LANES
            out_ref[:, lane : lane + LANES] = total_ref[h, c : c + 1].astype(jnp.bfloat16)
    gate = total_ref[0, rows : rows + 1] + total_ref[0, rows + 1 : rows + 2]
    gate_ref[...] = gate[:, 0 : gate_ref.shape[1]]


def padded_rows(width):
    return -(-(width // HALVES // LANES + 2) // 16) * 16


def on_device(nodes, locals_, tokens, out_grad, gate_prob, dest_node, w_gate, w_up, w_down):
    width, units = w_gate.shape[1:]
    weights = 6 * width * units
    rows = nodes * locals_ * 2 * HALVES * padded_rows(width) * LANES * 10
    small = (
        tokens.shape[0] == 1
        and gate_prob.shape[1] == locals_
        and locals_ % 2 == 0
        and width % (HALVES * COLUMNS) == 0
        and width % (16 * PIECES) == 0
        and units % TILE == 0
        and weights + rows < 40 << 20
    )
    plan = functools.partial(fused, nodes, locals_) if small else routed
    return plan(tokens, out_grad, gate_prob, dest_node, w_gate, w_up, w_down)


def solution(mesh):
    split = ("node", "local")
    return jax.shard_map(
        functools.partial(on_device, mesh.shape["node"], mesh.shape["local"]),
        mesh=mesh,
        in_specs=(P(split, None),) * 4 + (P(split, None, None),) * 3,
        out_specs=(P(split, None), P(split, None)),
        check_vma=False,
    )
```
